256 devices in a mesh: section: 16 (over x_hi, y, core), tp: 8 (over z), dp: 2 (over x_lo).
Axes of the slice: x: 4 (x_hi: 2, x_lo: 2; x = x_hi * 2 + x_lo), y: 4, z: 8, core: 2. Of those that a mesh axis runs over, the one named last changes fastest.
Arguments:
- act_first: bfloat16 [16, 128, 4096], P('section', 'dp', 'tp'), may hold values from -6 to 6
- act_fresh: bfloat16 [2, 128, 4096], P(None, 'dp', 'tp'), may hold values from -6 to 6
- grad_first: bfloat16 [16, 128, 4096], P('section', 'dp', 'tp'), may hold values from -6 to 6
- grad_fresh: bfloat16 [2, 128, 4096], P(None, 'dp', 'tp'), may hold values from -6 to 6
- stash_values: bfloat16 [16, 3, 128, 4096], P('section', None, 'dp', 'tp'), may hold values from -448 to 448
- stash_scales: bfloat16 [16, 3, 128, 32], P('section', None, 'dp', 'tp'), may hold values from 0.00049972534 to 0.0059814453
- gains: float32 [16, 4096], P('section'), may hold values from 0.1 to 1.9
- w_in: bfloat16 [16, 4096, 4096], P('section', 'dp', 'tp'), may hold values from -0.09375 to 0.09375
- w_out: bfloat16 [16, 4096, 4096], P('section', 'tp', 'dp'), may hold values from -0.09375 to 0.09375
Outputs:
- act_out: bfloat16 [16, 128, 4096], P('section', 'dp', 'tp')
- grad_out: bfloat16 [16, 128, 4096], P('section', 'dp', 'tp')
- stash_out_values: bfloat16 [16, 3, 128, 4096], P('section', None, 'dp', 'tp')
- stash_out_scales: bfloat16 [16, 3, 128, 32], P('section', None, 'dp', 'tp')
- grad_in_w: bfloat16 [16, 4096, 4096], P('section', 'dp', 'tp')
- grad_out_w: bfloat16 [16, 4096, 4096], P('section', 'tp', 'dp')
- grad_gain: float32 [16, 4096], P('section', ('tp', 'dp'))
The draws below stay inside these ranges and needn't reach their ends.
All inputs are finite; a program needn't handle non-finite values.
Results may differ from the reference program's by a relative error of at most 0.035.
Values may be sent and summed in bfloat16 or wider, within the bound.
A program may use at most 128 MiB of HBM per device.

```python
import math
import jax
import jax.numpy as jnp
from jax import lax

D = 4096
INNER = 4096
BLOCK = 128
TICKS = 3
TOK = 64
SECTIONS = 16
TOKENS = 128
TP_PARTS = 8
DP_PARTS = 2


def block_scale(key, dims, cuts, least, largest):
    factor_of, own = 1.0, jax.random.fold_in(key, 6)
    for position, blocks in cuts:
        draws = jnp.exp(jax.random.uniform(jax.random.fold_in(own, position), (blocks,), jnp.float32, least / len(cuts), largest / len(cuts)))
        factor_of = factor_of * jnp.repeat(draws, dims[position] // blocks).reshape([-1 if axis == position else 1 for axis in range(len(dims))])
    return factor_of


def centred(rng, extent, spread, reach, shards=(), held_as=jnp.bfloat16):
    array = spread * jax.random.normal(rng, extent, jnp.float32)
    if shards:
        array = array * block_scale(rng, extent, shards, -0.22, 0.18)
    return jnp.clip(array, -reach, reach).astype(held_as)


def setup_inputs(seed: int = 0) -> dict:
    arg_keys = jax.random.split(jax.random.key(seed), 10)
    return {
        "act_first": centred(arg_keys[0], (SECTIONS, TOKENS, D), 1.0, 6.0, ((0, 16), (1, 2), (2, 8))),
        "act_fresh": centred(arg_keys[1], (TICKS - 1, TOKENS, D), 1.0, 6.0, ((1, 2), (2, 8))),
        "grad_first": centred(arg_keys[2], (SECTIONS, TOKENS, D), 1.0, 6.0, ((0, 16), (1, 2), (2, 8))),
        "grad_fresh": centred(arg_keys[3], (TICKS - 1, TOKENS, D), 1.0, 6.0, ((1, 2), (2, 8))),
        "stash_values": jnp.clip(jax.random.uniform(arg_keys[4], (SECTIONS, TICKS, TOKENS, D), jnp.float32, -448.0, 448.0) * block_scale(arg_keys[4], (SECTIONS, TICKS, TOKENS, D), ((0, 16), (2, 2), (3, 8)), -0.4, 0.0), -448.0, 448.0).astype(jnp.bfloat16),
        "stash_scales": jnp.clip(jnp.exp(math.log(0.0059814453) - 2.482359 * jax.random.uniform(arg_keys[5], (SECTIONS, TICKS, TOKENS, D // BLOCK), jnp.float32) ** block_scale(arg_keys[5], (SECTIONS, TICKS, TOKENS, D // BLOCK), ((0, 16), (2, 2), (3, 8)), -0.2, 0.2)), 0.00049972534, 0.0059814453).astype(jnp.bfloat16),
        "gains": jnp.clip(1.0 + 0.18 * jax.random.normal(arg_keys[6], (SECTIONS, D), jnp.float32), 0.1, 1.9),
        "w_in": centred(arg_keys[7], (SECTIONS, D, INNER), D ** -0.5, 0.09375, ((0, 16), (1, 2), (2, 8))),
        "w_out": centred(arg_keys[8], (SECTIONS, INNER, D), INNER ** -0.5, 0.09375, ((0, 16), (1, 8), (2, 2))),
    }


norm_eps = 1e-05
quant_top = 448.0
scale_eps = 1e-06

def quantize(inputs):
    blocks = inputs.astype(jnp.float32).reshape(inputs.shape[:-1] + (inputs.shape[-1] // BLOCK, BLOCK))
    scales = (lax.optimization_barrier(jnp.max(jnp.abs(blocks), axis=-1)) / quant_top + scale_eps).astype(jnp.bfloat16)
    values = (blocks / scales.astype(jnp.float32)[..., None]).astype(jnp.bfloat16)
    return (values.reshape(inputs.shape), scales)

def dequantize(values, scales):
    blocks = values.astype(jnp.float32).reshape(values.shape[:-1] + (values.shape[-1] // BLOCK, BLOCK))
    return (blocks * scales.astype(jnp.float32)[..., None]).reshape(values.shape).astype(jnp.bfloat16)

def grouped_sum(left_rows, right_rows):
    group_width = left_rows.shape[1] // TP_PARTS
    running = jnp.zeros((left_rows.shape[0], right_rows.shape[1]), jnp.float32)
    for group_index in range(TP_PARTS):
        low = group_index * group_width
        piece_sum = jnp.dot(left_rows[:, low:low + group_width], right_rows[low:low + group_width], preferred_element_type=jnp.float32)
        rounded = lax.optimization_barrier(piece_sum.astype(jnp.bfloat16))
        running = running + rounded.astype(jnp.float32)
    return running

def forward_layer(inputs, gain_row, weight_in, weight_out):
    widened = inputs.astype(jnp.float32)
    inv_rms = lax.rsqrt(lax.optimization_barrier(jnp.mean(widened * widened, axis=-1, keepdims=True)) + norm_eps)
    normed = (widened * inv_rms * gain_row).astype(jnp.bfloat16)
    pre_act = jnp.dot(normed, weight_in, preferred_element_type=jnp.float32)
    hidden = (pre_act * jax.nn.sigmoid(pre_act)).astype(jnp.bfloat16)
    return (widened + grouped_sum(hidden, weight_out)).astype(jnp.bfloat16)

def backward_layer(restored, upstream, gain_row, weight_in, weight_out):
    widened = restored.astype(jnp.float32)
    inv_rms = lax.rsqrt(lax.optimization_barrier(jnp.mean(widened * widened, axis=-1, keepdims=True)) + norm_eps)
    unit_rows = widened * inv_rms
    normed = (unit_rows * gain_row).astype(jnp.bfloat16)
    pre_act = jnp.dot(normed, weight_in, preferred_element_type=jnp.float32)
    gate_prob = jax.nn.sigmoid(pre_act)
    hidden = (pre_act * gate_prob).astype(jnp.bfloat16)
    grad_hidden = jnp.dot(upstream, weight_out.T, preferred_element_type=jnp.float32)
    grad_pre = (grad_hidden * gate_prob * (1.0 + pre_act * (1.0 - gate_prob))).astype(jnp.bfloat16)
    grad_normed = grouped_sum(grad_pre, weight_in.T)
    grad_unit = grad_normed * gain_row
    center = lax.optimization_barrier(jnp.mean(grad_unit * unit_rows, axis=-1, keepdims=True))
    grad_input = (upstream.astype(jnp.float32) + inv_rms * (grad_unit - unit_rows * center)).astype(jnp.bfloat16)
    return (grad_input, normed, hidden, grad_pre, grad_normed * unit_rows)

def parted_product(left_list, right_list):
    running = jnp.zeros((left_list[0].shape[1], right_list[0].shape[1]), jnp.float32)
    for part_index in range(DP_PARTS):
        low = part_index * TOK
        left_all = jnp.concatenate([item[low:low + TOK] for item in left_list], axis=0)
        right_all = jnp.concatenate([item[low:low + TOK] for item in right_list], axis=0)
        piece_sum = jnp.dot(left_all.T, right_all, preferred_element_type=jnp.float32)
        running = running + lax.optimization_barrier(piece_sum.astype(jnp.bfloat16)).astype(jnp.float32)
    return running

def parted_rows(term_list):
    running = jnp.zeros((term_list[0].shape[1],), jnp.float32)
    for part_index in range(DP_PARTS):
        low = part_index * TOK
        piece_sum = jnp.zeros((term_list[0].shape[1],), jnp.float32)
        for item in term_list:
            piece_sum = piece_sum + lax.optimization_barrier(jnp.sum(item[low:low + TOK], axis=0))
        running = running + lax.optimization_barrier(piece_sum.astype(jnp.bfloat16)).astype(jnp.float32)
    return running

def reference(act_first, act_fresh, grad_first, grad_fresh, stash_values, stash_scales, gains, w_in, w_out):
    grad_scale = 1.0 / math.sqrt(TICKS * TOKENS)
    current = [act_first[section_index] for section_index in range(SECTIONS)]
    arriving = [grad_first[section_index] for section_index in range(SECTIONS)]
    new_values = [[None] * TICKS for section_index in range(SECTIONS)]
    new_scales = [[None] * TICKS for section_index in range(SECTIONS)]
    saved = [[] for section_index in range(SECTIONS)]
    outputs = current
    grad_inputs = arriving
    for tick_index in range(TICKS):
        outputs = []
        grad_inputs = []
        for section_index in range(SECTIONS):
            mirror_row = SECTIONS - 1 - section_index
            values, scales = quantize(current[section_index])
            new_values[mirror_row][tick_index] = values
            new_scales[mirror_row][tick_index] = scales
            outputs.append(forward_layer(current[section_index], gains[section_index], w_in[section_index], w_out[section_index]))
            restored = dequantize(stash_values[mirror_row, tick_index], stash_scales[mirror_row, tick_index])
            grad_input, normed, hidden, grad_pre, gain_term = backward_layer(restored, arriving[section_index], gains[section_index], w_in[section_index], w_out[section_index])
            grad_inputs.append(grad_input)
            saved[section_index].append((normed, hidden, grad_pre, arriving[section_index], gain_term))
        if tick_index + 1 < TICKS:
            current = [act_fresh[tick_index]] + outputs[:-1]
            arriving = grad_inputs[1:] + [grad_fresh[tick_index]]
    in_grads, out_grads, gain_grads = ([], [], [])
    for section_index in range(SECTIONS):
        items = saved[section_index]
        in_term = parted_product([item[0] for item in items], [item[2] for item in items])
        out_term = parted_product([item[1] for item in items], [item[3] for item in items])
        gain_term = parted_rows([item[4] for item in items])
        in_grads.append((in_term * grad_scale).astype(jnp.bfloat16))
        out_grads.append((out_term * grad_scale).astype(jnp.bfloat16))
        gain_grads.append(gain_term * grad_scale)
    stash_out_values = jnp.stack([jnp.stack(row) for row in new_values])
    stash_out_scales = jnp.stack([jnp.stack(row) for row in new_scales])
    return (jnp.stack(outputs), jnp.stack(grad_inputs), stash_out_values, stash_out_scales, jnp.stack(in_grads), jnp.stack(out_grads), jnp.stack(gain_grads))
```

```python
import functools
import math

import jax
import jax.numpy as jnp
from jax import lax
from jax.experimental import pallas as pl
from jax.experimental.pallas import tpu as pltpu
from jax.sharding import PartitionSpec as P

MESH = pl.DeviceIdType.MESH
BLOCK = 128
EPS = 1e-05
QUANT_TOP = 448.0
SCALE_EPS = 1e-06
F32 = jnp.float32
BF16 = jnp.bfloat16

TP = 8
DP = 2

NN = (((1,), (0,)), ((), ()))
NT = (((1,), (1,)), ((), ()))
TN = (((0,), (0,)), ((), ()))


def mm(a, b, dims):
    return lax.dot_general(a, b, dims, preferred_element_type=F32)


def sigmoid(x):
    return 1.0 / (1.0 + jnp.exp(-x))


def column_of(tile, rows):
    wide = jnp.concatenate([tile] * (rows // 8), axis=0)
    return wide.T[:, 0:1]


def tile_of(column, rows):
    return jnp.broadcast_to(column, (rows, rows)).T[0:8, :]


def kernel(
    sections, ticks, tok, width, half, inner,
    act_first, act_fresh, grad_first, grad_fresh, stash_values, stash_scales, gains, w_in_hbm, w_out_hbm,
    act_out, grad_out, out_values, out_scales, grad_in_w, grad_out_w, grad_gain,
    w_in, w_out, gain,
    A, U, R, rest, raw,
    Fp, Bp, Fr, Br, Fs, Bs, Fl, Bl,
    xs, xr, xsum_s, xsum_r,
    b_pre, b_sg, BN, BH, GP, unit_scale,
    gacc, gpieces, gsum, grecv,
    fin_a, fin_g,
    lsem, ssem, rsem,
):
    s = lax.axis_index("section")
    t = lax.axis_index("tp")
    d = lax.axis_index("dp")
    tokens = DP * tok
    rows = tokens // TP
    hw = half // 2
    model = half * DP
    fwd_width, bwd_width = half, half + 128

    quarter = lax.rem(t, 4)
    side = t // 4
    last = sections - 1

    def dev(sec, tp, dp):
        return {"section": sec, "tp": tp, "dp": dp}

    def ztp(by):
        return lax.rem(t + (by + TP), TP)

    counts = {"s": 0}
    names = {}
    pending = []

    def slot(key):
        if key not in names:
            names[key] = len(names)
        return rsem.at[names[key]]

    def push(src, dst, key, device, cond=None, is_self=None):
        sem = ssem.at[counts["s"]]
        counts["s"] += 1
        arrive = slot(key)
        copy = pltpu.make_async_remote_copy(
            src_ref=src, dst_ref=dst, send_sem=sem, recv_sem=arrive, device_id=device, device_id_type=MESH
        )
        go = cond
        if is_self is not None:
            own = is_self if cond is None else jnp.logical_and(cond, is_self)
            go = jnp.logical_not(is_self) if cond is None else jnp.logical_and(cond, jnp.logical_not(is_self))

            @pl.when(own)
            def _():
                pltpu.make_async_copy(src, dst, arrive).start()

        if go is None:
            copy.start()
        else:
            pl.when(go)(copy.start)
        pending.append((copy, go))

    def arrived(ref, key):
        pltpu.make_async_copy(ref, ref, slot(key)).wait()

    load_in = pltpu.make_async_copy(w_in_hbm.at[0], w_in, lsem.at[0])
    load_out = pltpu.make_async_copy(w_out_hbm.at[0], w_out, lsem.at[1])
    load_in.start()
    load_out.start()

    barrier = pltpu.get_barrier_semaphore()

    def greet(device, cond=None):
        def signal():
            pl.semaphore_signal(barrier, inc=1, device_id=device, device_id_type=MESH)

        if cond is None:
            signal()
        else:
            pl.when(cond)(signal)

    def is_own(i):
        return jnp.logical_and(side == d, quarter == i)

    up, down = s < last, s > 0
    for by in (1, -1, 2, -2):
        greet(dev(s, ztp(by), d))
    greet(dev(s, t, 1 - d))
    greet(dev(s + 1, t, d), up)
    greet(dev(s - 1, t, d), down)
    greet(dev(last - s, t, d))
    for i in range(4):
        greet(dev(s, 4 * d + i, side), jnp.logical_not(is_own(i)))
        greet(dev(last - s, 4 * d + i, side))
        greet(dev(last - 1 - s, 4 * d + i, side), jnp.logical_and(up, jnp.logical_not(jnp.logical_and(s == last // 2, is_own(i)))))
    self_side = (side == d).astype(jnp.int32)
    expect = (
        4 + 1 + up.astype(jnp.int32) + down.astype(jnp.int32) + 1
        + (4 - self_side) + 4
        + up.astype(jnp.int32) * (4 - self_side * (s == last // 2).astype(jnp.int32))
    )

    for k in range(ticks):
        for b in range(width // BLOCK):
            cols = pl.ds(b * BLOCK, BLOCK)
            scale = stash_scales[0, k, :, b : b + 1].astype(F32)
            rest[k, :, cols] = (stash_values[0, k, :, cols].astype(F32) * scale).astype(BF16)
    gain[...] = gains[:, pl.ds(pl.multiple_of(d * half, half), half)]

    pl.semaphore_wait(barrier, expect)

    piece_cols = pl.ds(pl.multiple_of(quarter * width, width), width)

    def to_slots(src, dst, key, sec, cond=None, other=False):
        for i in range(4):
            push(
                src.at[pl.ds(rows * i, rows)], dst.at[pl.ds(0, rows), piece_cols], key,
                dev(sec, 4 * d + i, side), cond, None if other else is_own(i),
            )

    def to_blocks(src, dst, key, sec, cond=None, own=None):
        for i in range(4):
            mine = is_own(i) if own is None else jnp.logical_and(own, is_own(i))
            push(
                src.at[pl.ds(0, rows), pl.ds(i * width, width)],
                dst.at[pl.ds(pl.multiple_of(quarter * rows, rows), rows)], key,
                dev(sec, 4 * d + i, side), cond, mine,
            )

    to_slots(act_first.at[0], A.at[0], ("A", 0), s)
    to_slots(grad_first.at[0], U.at[0], ("U", 0), s)
    for k in range(ticks):
        to_slots(rest.at[k], R.at[k], ("R", k), last - s, other=True)
    push(act_first.at[0], raw.at[0], ("raw", 0), dev(last - s, t, d))
    for k in range(1, ticks):
        to_slots(act_fresh.at[k - 1], A.at[k], ("A", k), s, s == 0)
        to_slots(grad_fresh.at[k - 1], U.at[k], ("U", k), s, s == last)

    def rows_of(j):
        return pl.ds(rows * j, rows)

    def gather_start(X, key):
        arrived(X.at[rows_of(0)], key)
        own = X.at[rows_of(0)]
        push(own, X.at[rows_of(2)], key + (2,), dev(s, ztp(-2), d))
        push(own, X.at[rows_of(6)], key + (6,), dev(s, ztp(2), d))
        push(own, X.at[rows_of(1)], key + (1,), dev(s, ztp(-1), d))
        push(own, X.at[rows_of(7)], key + (7,), dev(s, ztp(1), d))

    def gather_mid(X, key):
        arrived(X.at[rows_of(2)], key + (2,))
        push(X.at[rows_of(2)], X.at[rows_of(3)], key + (3,), dev(s, ztp(-1), d))
        push(X.at[rows_of(2), pl.ds(0, hw)], X.at[rows_of(4), pl.ds(0, hw)], key + (4,), dev(s, ztp(-2), d))
        arrived(X.at[rows_of(6)], key + (6,))
        push(X.at[rows_of(6)], X.at[rows_of(5)], key + (5,), dev(s, ztp(1), d))
        push(X.at[rows_of(6), pl.ds(hw, hw)], X.at[rows_of(4), pl.ds(hw, hw)], key + (8,), dev(s, ztp(2), d))

    def gather_end(X, key):
        for j in (1, 7, 3, 5):
            arrived(X.at[rows_of(j)], key + (j,))
        arrived(X.at[rows_of(4), pl.ds(0, hw)], key + (4,))
        arrived(X.at[rows_of(4), pl.ds(hw, hw)], key + (8,))

    def sum_start(Pk, Rk, w, key):
        push(Pk.at[rows_of(3)], Rk.at[0], key + (0,), dev(s, ztp(1), d))
        push(Pk.at[rows_of(5)], Rk.at[1], key + (1,), dev(s, ztp(-1), d))
        push(Pk.at[rows_of(4), pl.ds(0, hw)], Rk.at[2, :, pl.ds(0, hw)], key + (2,), dev(s, ztp(2), d))
        push(Pk.at[rows_of(4), pl.ds(hw, w - hw)], Rk.at[3, :, pl.ds(hw, w - hw)], key + (3,), dev(s, ztp(-2), d))
        push(Pk.at[rows_of(1)], Rk.at[4], key + (4,), dev(s, ztp(1), d))
        push(Pk.at[rows_of(7)], Rk.at[5], key + (5,), dev(s, ztp(-1), d))

    def sum_mid(Pk, Rk, Sk, w, key):
        arrived(Rk.at[0], key + (0,))
        arrived(Rk.at[2, :, pl.ds(0, hw)], key + (2,))
        lo, hi = pl.ds(0, hw), pl.ds(hw, w - hw)
        Sk[0, :, lo] = (
            Pk[rows_of(2), lo].astype(F32) + Rk[0, :, lo].astype(F32) + Rk[2, :, lo].astype(F32)
        ).astype(BF16)
        Sk[0, :, hi] = (Pk[rows_of(2), hi].astype(F32) + Rk[0, :, hi].astype(F32)).astype(BF16)
        push(Sk.at[0], Rk.at[6], key + (6,), dev(s, ztp(2), d))
        arrived(Rk.at[1], key + (1,))
        arrived(Rk.at[3, :, pl.ds(hw, w - hw)], key + (3,))
        Sk[1, :, hi] = (
            Pk[rows_of(6), hi].astype(F32) + Rk[1, :, hi].astype(F32) + Rk[3, :, hi].astype(F32)
        ).astype(BF16)
        Sk[1, :, lo] = (Pk[rows_of(6), lo].astype(F32) + Rk[1, :, lo].astype(F32)).astype(BF16)
        push(Sk.at[1], Rk.at[7], key + (7,), dev(s, ztp(-2), d))

    def sum_end(Pk, Rk, key):
        for j in (4, 5, 6, 7):
            arrived(Rk.at[j], key + (j,))
        total = Pk[rows_of(0)].astype(F32)
        for j in (4, 5, 6, 7):
            total = total + Rk[j].astype(F32)
        return total

    def swap_send(i, key):
        push(xs.at[i], xr.at[i], key, dev(s, t, 1 - d))

    def swap_sum_send(i, key):
        push(xsum_s.at[i], xsum_r.at[i], key + ("q",), dev(s, t, 1 - d))

    def project(X, i, key):
        wide = X[...].astype(F32)
        xsum_s[i] = tile_of(jnp.sum(wide * wide, axis=-1, keepdims=True), tokens)
        swap_sum_send(i, key)
        part = mm((wide * gain[...]).astype(BF16), w_in[...], NN)
        xs[i] = part.astype(BF16)
        swap_send(i, key)
        return part

    def projected(part, i, key):
        arrived(xsum_r.at[i], key + ("q",))
        arrived(xr.at[i], key)
        total = column_of(xsum_s[i] + xsum_r[i], tokens)
        inv = lax.rsqrt(total * (1.0 / model) + EPS)
        return inv * (part + xr[i].astype(F32)), inv

    def restore_project(k):
        return project(R.at[k], 3 * k + 1, ("xb", k))

    def restore_finish(k, part):
        pre, inv = projected(part, 3 * k + 1, ("xb", k))
        gate = sigmoid(pre)
        unit_scale[k] = jnp.broadcast_to(inv, (tokens, BLOCK))
        b_pre[k] = pre
        b_sg[k] = gate * (1.0 + pre * (1.0 - gate))
        BH[pl.ds(k * tokens, tokens)] = (pre * gate).astype(BF16)
        BN[pl.ds(k * tokens, tokens)] = (R[k].astype(F32) * inv * gain[...]).astype(BF16)

    def quantize(k):
        blocks = raw[k].astype(F32)
        scales = []
        for b in range(width // BLOCK):
            block = blocks[:, b * BLOCK : (b + 1) * BLOCK]
            top = jnp.max(jnp.abs(block), axis=-1, keepdims=True)
            scale = (top / QUANT_TOP + SCALE_EPS).astype(BF16)
            out_values[0, k, :, pl.ds(b * BLOCK, BLOCK)] = (block / scale.astype(F32)).astype(BF16)
            scales.append(scale.astype(F32))
        out_scales[0, k] = jnp.concatenate(scales, axis=1).astype(BF16)

    scale_out = 1.0 / math.sqrt(ticks * tokens)

    for k in range(ticks):
        gather_start(A.at[k], ("A", k))
        gather_start(U.at[k], ("U", k))
        if k == 0:
            gather_start(R.at[k], ("R", k))
            load_in.wait()
            load_out.wait()
        gather_mid(A.at[k], ("A", k))
        gather_mid(U.at[k], ("U", k))
        if k == 0:
            gather_mid(R.at[k], ("R", k))
        gather_end(A.at[k], ("A", k))
        f_part = project(A.at[k], 3 * k, ("xf", k))
        gather_end(U.at[k], ("U", k))
        g_part = mm(U[k], w_out[...], NT)
        xs[3 * k + 2] = g_part.astype(BF16)
        swap_send(3 * k + 2, ("xg", k))
        if k == 0:
            gather_end(R.at[k], ("R", k))
            r_part = restore_project(k)
        if k + 1 < ticks:
            gather_start(R.at[k + 1], ("R", k + 1))
        f_pre, _ = projected(f_part, 3 * k, ("xf", k))
        hidden = (f_pre * sigmoid(f_pre)).astype(BF16)
        Fp[k] = mm(hidden, w_out[...], NN).astype(BF16)
        sum_start(Fp.at[k], Fr.at[k], fwd_width, ("F", k))
        if k == 0:
            restore_finish(k, r_part)
        arrived(xr.at[3 * k + 2], ("xg", k))
        grad_pre = ((g_part + xr[3 * k + 2].astype(F32)) * b_sg[k]).astype(BF16)
        GP[pl.ds(k * tokens, tokens)] = grad_pre
        center = jnp.sum(grad_pre.astype(F32) * b_pre[k], axis=-1, keepdims=True)
        center_hi = center.astype(BF16).astype(F32)
        lane = lax.broadcasted_iota(jnp.int32, (tokens, BLOCK), 1)
        Bp[k, :, pl.ds(half, BLOCK)] = jnp.where(lane < BLOCK // 2, center_hi, center - center_hi).astype(BF16)
        Bp[k, :, pl.ds(0, half)] = mm(grad_pre, w_in[...], NT).astype(BF16)
        sum_start(Bp.at[k], Br.at[k], bwd_width, ("B", k))
        if k + 1 < ticks:
            gather_mid(R.at[k + 1], ("R", k + 1))
        sum_mid(Fp.at[k], Fr.at[k], Fs.at[k], fwd_width, ("F", k))
        sum_mid(Bp.at[k], Br.at[k], Bs.at[k], bwd_width, ("B", k))
        if k + 1 < ticks:
            gather_end(R.at[k + 1], ("R", k + 1))
            r_part = restore_project(k + 1)
        leaving = (A[k, rows_of(0)].astype(F32) + sum_end(Fp.at[k], Fr.at[k], ("F", k))).astype(BF16)
        Fl[k] = leaving
        if k + 1 < ticks:
            push(Fl.at[k], A.at[k + 1, rows_of(0)], ("A", k + 1), dev(s + 1, t, d), up)
            to_blocks(Fl.at[k], raw.at[k + 1], ("raw", k + 1), last - 1 - s, up, s == last // 2)
        else:
            to_blocks(Fl.at[k], fin_a, ("fin_a",), s)
        total = sum_end(Bp.at[k], Br.at[k], ("B", k))
        grad_normed = total[:, :half]
        center = total[:, half : half + 1] + total[:, half + BLOCK // 2 : half + BLOCK // 2 + 1]
        inv = unit_scale[k, rows_of(0)][:, 0:1]
        unit = R[k, rows_of(0)].astype(F32) * inv
        grads = grad_normed * gain[...] - unit * (center * (1.0 / model))
        leaving = (U[k, rows_of(0)].astype(F32) + inv * grads).astype(BF16)
        Bl[k] = leaving
        if k + 1 < ticks:
            push(Bl.at[k], U.at[k + 1, rows_of(0)], ("U", k + 1), dev(s - 1, t, d), down)
        else:
            to_blocks(Bl.at[k], fin_g, ("fin_g",), s)
        terms = grad_normed * unit
        terms = terms[0:8] + terms[8:16]
        gacc[...] = terms if k == 0 else gacc[...] + terms
        if k + 1 < ticks:
            restore_finish(k + 1, r_part)

    for i in range(4):
        push(
            gacc.at[:, pl.ds(i * width, width)], gpieces.at[quarter], ("gp",), dev(s, 4 * d + i, side), None, is_own(i)
        )
    step = 256
    for i in range(half // step):
        cols = pl.ds(i * step, step)
        grad_in_w[0, cols, :] = (mm(BN[:, cols], GP[...], TN) * scale_out).astype(BF16)
    arrived(gpieces, ("gp",))
    group = jnp.sum(gpieces[0] + gpieces[1] + gpieces[2] + gpieces[3], axis=0, keepdims=True)
    gsum[...] = jnp.broadcast_to(group.astype(BF16).astype(F32), gsum.shape)
    part_width = width // DP
    mine = pl.ds(pl.multiple_of(d * part_width, part_width), part_width)
    theirs = pl.ds(pl.multiple_of((1 - d) * part_width, part_width), part_width)
    push(gsum.at[:, theirs], grecv, ("gx",), dev(s, t, 1 - d))
    for i in range(inner // step):
        cols = pl.ds(i * step, step)
        total = mm(BH[pl.ds(0, tokens), cols], U[0], TN)
        for k in range(1, ticks):
            total = total + mm(BH[pl.ds(k * tokens, tokens), cols], U[k], TN)
        grad_out_w[0, cols, :] = (total * scale_out).astype(BF16)
    arrived(raw.at[0], ("raw", 0))
    for k in range(1, ticks):

        @pl.when(s < last)
        def _():
            arrived(raw.at[k], ("raw", k))

        @pl.when(s == last)
        def _():
            raw[k] = act_fresh[k - 1]

    for k in range(ticks):
        quantize(k)
    arrived(fin_a, ("fin_a",))
    act_out[0] = fin_a[...]
    arrived(fin_g, ("fin_g",))
    grad_out[0] = fin_g[...]
    arrived(grecv, ("gx",))
    grad_gain[...] = ((gsum[:, mine] + grecv[...]) * scale_out)[0:1]
    for copy, cond in pending:
        if cond is None:
            copy.wait_send()
        else:
            pl.when(cond)(copy.wait_send)


def local(act_first, act_fresh, grad_first, grad_fresh, stash_values, stash_scales, gains, w_in, w_out):
    sections = lax.axis_size("section")
    ticks = act_fresh.shape[0] + 1
    tok, width = act_first.shape[1:]
    half, inner = w_in.shape[1:]
    tokens = tok * DP
    rows = tokens // TP
    vmem = pl.BlockSpec(memory_space=pltpu.VMEM)
    hbm = pl.BlockSpec(memory_space=pl.ANY)
    bw = half + BLOCK
    V = pltpu.VMEM
    return pl.pallas_call(
        functools.partial(kernel, sections, ticks, tok, width, half, inner),
        out_shape=(
            jax.ShapeDtypeStruct(act_first.shape, BF16),
            jax.ShapeDtypeStruct(grad_first.shape, BF16),
            jax.ShapeDtypeStruct(stash_values.shape, BF16),
            jax.ShapeDtypeStruct(stash_scales.shape, BF16),
            jax.ShapeDtypeStruct(w_in.shape, BF16),
            jax.ShapeDtypeStruct(w_out.shape, BF16),
            jax.ShapeDtypeStruct((1, width // DP), F32),
        ),
        in_specs=[vmem] * 7 + [hbm] * 2,
        out_specs=(vmem,) * 7,
        scratch_shapes=[
            V((half, inner), BF16),
            V((inner, half), BF16),
            V((1, half), F32),
            V((ticks, tokens, half), BF16),
            V((ticks, tokens, half), BF16),
            V((ticks, tokens, half), BF16),
            V((ticks, tok, width), BF16),
            V((ticks, tok, width), BF16),
            V((ticks, tokens, half), BF16),
            V((ticks, tokens, bw), BF16),
            V((ticks, 8, rows, half), BF16),
            V((ticks, 8, rows, bw), BF16),
            V((ticks, 2, rows, half), BF16),
            V((ticks, 2, rows, bw), BF16),
            V((ticks, rows, half), BF16),
            V((ticks, rows, half), BF16),
            V((3 * ticks, tokens, inner), BF16),
            V((3 * ticks, tokens, inner), BF16),
            V((3 * ticks, 8, tokens), F32),
            V((3 * ticks, 8, tokens), F32),
            V((ticks, tokens, inner), F32),
            V((ticks, tokens, inner), F32),
            V((ticks * tokens, half), BF16),
            V((ticks * tokens, inner), BF16),
            V((ticks * tokens, inner), BF16),
            V((ticks, tokens, BLOCK), F32),
            V((8, half), F32),
            V((4, 8, width), F32),
            V((8, width), F32),
            V((8, width // DP), F32),
            V((tok, width), BF16),
            V((tok, width), BF16),
            pltpu.SemaphoreType.DMA((2,)),
            pltpu.SemaphoreType.DMA((224,)),
            pltpu.SemaphoreType.DMA((160,)),
        ],
        compiler_params=pltpu.CompilerParams(
            collective_id=1, has_side_effects=True, vmem_limit_bytes=56 * 2**20
        ),
        name="relay_window",
    )(act_first, act_fresh, grad_first, grad_fresh, stash_values, stash_scales, gains, w_in, w_out)


def solution(mesh):
    in_specs = (
        P("section", "dp", "tp"),
        P(None, "dp", "tp"),
        P("section", "dp", "tp"),
        P(None, "dp", "tp"),
        P("section", None, "dp", "tp"),
        P("section", None, "dp", "tp"),
        P("section", None),
        P("section", "dp", "tp"),
        P("section", "tp", "dp"),
    )
    out_specs = (
        P("section", "dp", "tp"),
        P("section", "dp", "tp"),
        P("section", None, "dp", "tp"),
        P("section", None, "dp", "tp"),
        P("section", "dp", "tp"),
        P("section", "tp", "dp"),
        P("section", ("tp", "dp")),
    )
    return jax.shard_map(local, mesh=mesh, in_specs=in_specs, out_specs=out_specs, check_vma=False)
```

```python
import functools
import math

import jax
import jax.numpy as jnp
from jax import lax
from jax.experimental import pallas as pl
from jax.experimental.pallas import tpu as pltpu
from jax.sharding import PartitionSpec as P

MESH = pl.DeviceIdType.MESH
scope = jax.named_scope
BLOCK = 128
EPS = 1e-05
QUANT_TOP = 448.0
SCALE_EPS = 1e-06
F32 = jnp.float32
BF16 = jnp.bfloat16

TP = 8
DP = 2

NN = (((1,), (0,)), ((), ()))
NT = (((1,), (1,)), ((), ()))
TN = (((0,), (0,)), ((), ()))


def mm(a, b, dims):
    return lax.dot_general(a, b, dims, preferred_element_type=F32)


def sigmoid(x):
    return 1.0 / (1.0 + jnp.exp(-x))


def column_of(tile, rows):
    wide = jnp.concatenate([tile] * (rows // 8), axis=0)
    return wide.T[:, 0:1]


def tile_of(column, rows):
    return jnp.broadcast_to(column, (rows, rows)).T[0:8, :]


def kernel(
    sections, ticks, tok, width, half, inner,
    act_first_h, act_fresh_h, grad_first_h, grad_fresh_h, stash_values_h, stash_scales_h, gains_h, w_in_h, w_out_h,
    act_out, grad_out, out_values, out_scales, grad_in_w, grad_out_w, grad_gain,
    act_first, act_fresh, grad_first, grad_fresh, stash_values, stash_scales, gain, w_in, w_out,
    A, U, R, rest, raw,
    Fp, Bp, Fr, Br, Fs, Bs, Fl, Bl,
    xs, xr, xsum_s, xsum_r,
    b_pre, b_sg, BN, BH, GP, unit_scale,
    gacc, gpieces,
    fin_a, fin_g,
    lsem, ssem, rsem,
):
    s = lax.axis_index("section")
    t = lax.axis_index("tp")
    d = lax.axis_index("dp")
    tokens = DP * tok
    rows = tokens // TP
    hw = half // 2
    model = half * DP
    fwd_width, bwd_width = half, half + 128

    quarter = lax.rem(t, 4)
    side = t // 4
    last = sections - 1

    def dev(sec, tp, dp):
        return {"section": sec, "tp": tp, "dp": dp}

    def ztp(by):
        return lax.rem(t + (by + TP), TP)

    counts = {"s": 0}
    names = {}
    pending = []

    def slot(key):
        if key not in names:
            names[key] = len(names)
        return rsem.at[names[key]]

    def push(src, dst, key, device, cond=None, is_self=None):
        sem = ssem.at[counts["s"]]
        counts["s"] += 1
        arrive = slot(key)
        copy = pltpu.make_async_remote_copy(
            src_ref=src, dst_ref=dst, send_sem=sem, recv_sem=arrive, device_id=device, device_id_type=MESH
        )
        go = cond
        if is_self is not None:
            own = is_self if cond is None else jnp.logical_and(cond, is_self)
            go = jnp.logical_not(is_self) if cond is None else jnp.logical_and(cond, jnp.logical_not(is_self))

            @pl.when(own)
            def _():
                pltpu.make_async_copy(src, dst, arrive).start()

        if go is None:
            copy.start()
        else:
            pl.when(go)(copy.start)
        pending.append((copy, go))

    def arrived(ref, key):
        pltpu.make_async_copy(ref, ref, slot(key)).wait()

    loads = []
    for i, (src, dst) in enumerate(
        (
            (stash_values_h.at[0], stash_values),
            (stash_scales_h.at[0], stash_scales),
            (act_first_h.at[0], act_first),
            (grad_first_h.at[0], grad_first),
            (gains_h.at[:, pl.ds(pl.multiple_of(d * half, half), half)], gain),
            (act_fresh_h, act_fresh),
            (grad_fresh_h, grad_fresh),
            (w_in_h.at[0], w_in),
            (w_out_h.at[0], w_out),
        )
    ):
        loads.append(pltpu.make_async_copy(src, dst, lsem.at[i]))
    for load in loads:
        load.start()

    barrier = pltpu.get_barrier_semaphore()

    def greet(device, cond=None):
        def signal():
            pl.semaphore_signal(barrier, inc=1, device_id=device, device_id_type=MESH)

        if cond is None:
            signal()
        else:
            pl.when(cond)(signal)

    def is_own(i):
        return jnp.logical_and(side == d, quarter == i)

    up, down = s < last, s > 0
    for by in (1, -1, 2, -2):
        greet(dev(s, ztp(by), d))
    greet(dev(s, t, 1 - d))
    for by in (0, 1, -1, 2, -2):
        greet(dev(s + 1, ztp(by), d), up)
        greet(dev(s - 1, ztp(by), d), down)
    greet(dev(last - s, t, d))
    for i in range(4):
        greet(dev(s, 4 * d + i, side), jnp.logical_not(is_own(i)))
        greet(dev(last - s, 4 * d + i, side))
        greet(dev(last - 1 - s, 4 * d + i, side), jnp.logical_and(up, jnp.logical_not(jnp.logical_and(s == last // 2, is_own(i)))))
    for i in range(TP):
        greet(dev(s, i, side), jnp.logical_not(jnp.logical_and(side == d, t == i)))
    self_side = (side == d).astype(jnp.int32)
    expect = (
        4 + 1 + 5 * up.astype(jnp.int32) + 5 * down.astype(jnp.int32) + 1
        + (4 - self_side) + 4 + (TP - self_side)
        + up.astype(jnp.int32) * (4 - self_side * (s == last // 2).astype(jnp.int32))
    )

    loads[0].wait()
    loads[1].wait()
    blocks = width // BLOCK
    eye = (
        lax.broadcasted_iota(jnp.int32, (blocks, blocks), 0) == lax.broadcasted_iota(jnp.int32, (blocks, blocks), 1)
    ).astype(F32).astype(BF16)
    for k in range(ticks):
        scale = mm(stash_scales[k], eye, TN)
        for b in range(blocks):
            cols = pl.ds(b * BLOCK, BLOCK)
            rest[k, :, cols] = (stash_values[k, :, cols].astype(F32) * scale[:, b : b + 1]).astype(BF16)

    loads[2].wait()
    loads[3].wait()
    pl.semaphore_wait(barrier, expect)

    piece_cols = pl.ds(pl.multiple_of(quarter * width, width), width)

    def to_slots(src, dst, key, sec, cond=None, other=False):
        for i in range(4):
            push(
                src.at[pl.ds(rows * i, rows)], dst.at[pl.ds(0, rows), piece_cols], key,
                dev(sec, 4 * d + i, side), cond, None if other else is_own(i),
            )

    def to_blocks(src, dst, key, sec, cond=None, own=None):
        for i in range(4):
            mine = is_own(i) if own is None else jnp.logical_and(own, is_own(i))
            push(
                src.at[pl.ds(0, rows), pl.ds(i * width, width)],
                dst.at[pl.ds(pl.multiple_of(quarter * rows, rows), rows)], key,
                dev(sec, 4 * d + i, side), cond, mine,
            )

    to_slots(act_first, A.at[0], ("A", 0), s)
    to_slots(rest.at[0], R.at[0], ("R", 0), last - s, other=True)
    to_slots(grad_first, U.at[0], ("U", 0), s)
    loads[4].wait()
    loads[5].wait()
    loads[6].wait()

    def later_slots(k):
        to_slots(rest.at[k], R.at[k], ("R", k), last - s, other=True)
        to_slots(act_fresh.at[k - 1], A.at[k], ("A", k), s, s == 0)
        to_slots(grad_fresh.at[k - 1], U.at[k], ("U", k), s, s == last)
        if k == 1:
            push(act_first, raw.at[0], ("raw", 0), dev(last - s, t, d))

    def rows_of(j):
        return pl.ds(rows * j, rows)

    def spread(src, X, key, sec, cond=None, whole=True):
        push(src, X.at[rows_of(2)], key + (2,), dev(sec, ztp(-2), d), cond)
        push(src, X.at[rows_of(6)], key + (6,), dev(sec, ztp(2), d), cond)
        push(src, X.at[rows_of(1)], key + (1,), dev(sec, ztp(-1), d), cond)
        push(src, X.at[rows_of(7)], key + (7,), dev(sec, ztp(1), d), cond)
        if whole:
            push(src, X.at[rows_of(0)], key, dev(sec, t, d), cond)

    def gather_start(X, key, cond=None):
        def first():
            arrived(X.at[rows_of(0)], key)

        if cond is None:
            first()
        else:
            pl.when(cond)(first)
        spread(X.at[rows_of(0)], X, key, s, cond, False)

    def chain(X, key, step):
        if step == 0:
            arrived(X.at[rows_of(0)], key)
            push(X.at[rows_of(0)], X.at[rows_of(1)], key + (1,), dev(s, ztp(-1), d))
            push(X.at[rows_of(0)], X.at[rows_of(7)], key + (7,), dev(s, ztp(1), d))
        elif step < 3:
            arrived(X.at[rows_of(step)], key + (step,))
            push(X.at[rows_of(step)], X.at[rows_of(step + 1)], key + (step + 1,), dev(s, ztp(-1), d))
            arrived(X.at[rows_of(8 - step)], key + (8 - step,))
            push(X.at[rows_of(8 - step)], X.at[rows_of(7 - step)], key + (7 - step,), dev(s, ztp(1), d))
        elif step == 3:
            arrived(X.at[rows_of(3)], key + (3,))
            push(X.at[rows_of(3), pl.ds(0, hw)], X.at[rows_of(4), pl.ds(0, hw)], key + (4,), dev(s, ztp(-1), d))
            arrived(X.at[rows_of(5)], key + (5,))
            push(X.at[rows_of(5), pl.ds(hw, hw)], X.at[rows_of(4), pl.ds(hw, hw)], key + (8,), dev(s, ztp(1), d))
        else:
            arrived(X.at[rows_of(4), pl.ds(0, hw)], key + (4,))
            arrived(X.at[rows_of(4), pl.ds(hw, hw)], key + (8,))

    def gather_mid(X, key):
        arrived(X.at[rows_of(2)], key + (2,))
        push(X.at[rows_of(2)], X.at[rows_of(3)], key + (3,), dev(s, ztp(-1), d))
        push(X.at[rows_of(2), pl.ds(0, hw)], X.at[rows_of(4), pl.ds(0, hw)], key + (4,), dev(s, ztp(-2), d))
        arrived(X.at[rows_of(6)], key + (6,))
        push(X.at[rows_of(6)], X.at[rows_of(5)], key + (5,), dev(s, ztp(1), d))
        push(X.at[rows_of(6), pl.ds(hw, hw)], X.at[rows_of(4), pl.ds(hw, hw)], key + (8,), dev(s, ztp(2), d))

    def gather_end(X, key, cond=None):
        if cond is not None:
            pl.when(cond)(lambda: arrived(X.at[rows_of(0)], key))
        for j in (1, 7, 3, 5):
            arrived(X.at[rows_of(j)], key + (j,))
        arrived(X.at[rows_of(4), pl.ds(0, hw)], key + (4,))
        arrived(X.at[rows_of(4), pl.ds(hw, hw)], key + (8,))

    def sum_start(Pk, Rk, w, key):
        push(Pk.at[rows_of(3)], Rk.at[0], key + (0,), dev(s, ztp(1), d))
        push(Pk.at[rows_of(5)], Rk.at[1], key + (1,), dev(s, ztp(-1), d))
        push(Pk.at[rows_of(4), pl.ds(0, hw)], Rk.at[2, :, pl.ds(0, hw)], key + (2,), dev(s, ztp(2), d))
        push(Pk.at[rows_of(4), pl.ds(hw, w - hw)], Rk.at[3, :, pl.ds(hw, w - hw)], key + (3,), dev(s, ztp(-2), d))
        push(Pk.at[rows_of(1)], Rk.at[4], key + (4,), dev(s, ztp(1), d))
        push(Pk.at[rows_of(7)], Rk.at[5], key + (5,), dev(s, ztp(-1), d))

    def sum_mid(Pk, Rk, Sk, w, key):
        arrived(Rk.at[0], key + (0,))
        arrived(Rk.at[2, :, pl.ds(0, hw)], key + (2,))
        lo, hi = pl.ds(0, hw), pl.ds(hw, w - hw)
        Sk[0, :, lo] = (
            Pk[rows_of(2), lo].astype(F32) + Rk[0, :, lo].astype(F32) + Rk[2, :, lo].astype(F32)
        ).astype(BF16)
        Sk[0, :, hi] = (Pk[rows_of(2), hi].astype(F32) + Rk[0, :, hi].astype(F32)).astype(BF16)
        push(Sk.at[0], Rk.at[6], key + (6,), dev(s, ztp(2), d))
        arrived(Rk.at[1], key + (1,))
        arrived(Rk.at[3, :, pl.ds(hw, w - hw)], key + (3,))
        Sk[1, :, hi] = (
            Pk[rows_of(6), hi].astype(F32) + Rk[1, :, hi].astype(F32) + Rk[3, :, hi].astype(F32)
        ).astype(BF16)
        Sk[1, :, lo] = (Pk[rows_of(6), lo].astype(F32) + Rk[1, :, lo].astype(F32)).astype(BF16)
        push(Sk.at[1], Rk.at[7], key + (7,), dev(s, ztp(-2), d))

    def sum_end(Pk, Rk, key):
        for j in (4, 5, 6, 7):
            arrived(Rk.at[j], key + (j,))
        total = Pk[rows_of(0)].astype(F32)
        for j in (4, 5, 6, 7):
            total = total + Rk[j].astype(F32)
        return total

    def swap_send(i, key):
        push(xs.at[i], xr.at[i], key, dev(s, t, 1 - d))

    def swap_sum_send(i, key):
        push(xsum_s.at[i], xsum_r.at[i], key + ("q",), dev(s, t, 1 - d))

    def project(X, i, key):
        wide = X[...].astype(F32)
        xsum_s[i] = tile_of(jnp.sum(wide * wide, axis=-1, keepdims=True), tokens)
        swap_sum_send(i, key)
        part = mm((wide * gain[...]).astype(BF16), w_in[...], NN)
        xs[i] = part.astype(BF16)
        swap_send(i, key)
        return part

    def projected(part, i, key):
        arrived(xsum_r.at[i], key + ("q",))
        arrived(xr.at[i], key)
        total = column_of(xsum_s[i] + xsum_r[i], tokens)
        inv = lax.rsqrt(total * (1.0 / model) + EPS)
        return inv * (part + xr[i].astype(F32)), inv

    def restore_project(k):
        return project(R.at[k], 3 * k + 1, ("xb", k))

    def restore_finish(k, part):
        pre, inv = projected(part, 3 * k + 1, ("xb", k))
        gate = sigmoid(pre)
        unit_scale[k] = jnp.broadcast_to(inv, (tokens, BLOCK))
        b_pre[k] = pre
        b_sg[k] = gate * (1.0 + pre * (1.0 - gate))
        BH[pl.ds(k * tokens, tokens)] = (pre * gate).astype(BF16)
        BN[pl.ds(k * tokens, tokens)] = (R[k].astype(F32) * inv * gain[...]).astype(BF16)

    def quantize(k):
        values = raw[k].astype(F32)
        scales = []
        for b in range(width // BLOCK):
            block = values[:, b * BLOCK : (b + 1) * BLOCK]
            top = jnp.max(jnp.abs(block), axis=-1, keepdims=True)
            scale = (top / QUANT_TOP + SCALE_EPS).astype(BF16)
            out_values[0, k, :, pl.ds(b * BLOCK, BLOCK)] = (block / scale.astype(F32)).astype(BF16)
            scales.append(scale.astype(F32))
        out_scales[0, k] = mm(eye, jnp.concatenate(scales, axis=1).astype(BF16), NT).astype(BF16)

    scale_out = 1.0 / math.sqrt(ticks * tokens)

    def forward_gather(k):
        gather_start(A.at[k], ("A", k), None if k == 0 else s == 0)

    def forward_pass_on(k):
        gather_mid(A.at[k], ("A", k))

    def forward_project(k):
        gather_end(A.at[k], ("A", k), None if k == 0 else s > 0)
        return project(A.at[k], 3 * k, ("xf", k))

    def forward_branch(k, part):
        pre, _ = projected(part, 3 * k, ("xf", k))
        hidden = (pre * sigmoid(pre)).astype(BF16)
        Fp[k] = mm(hidden, w_out[...], NN).astype(BF16)
        sum_start(Fp.at[k], Fr.at[k], fwd_width, ("F", k))

    def forward_sum(k):
        sum_mid(Fp.at[k], Fr.at[k], Fs.at[k], fwd_width, ("F", k))

    def forward_leave(k):
        Fl[k] = (A[k, rows_of(0)].astype(F32) + sum_end(Fp.at[k], Fr.at[k], ("F", k))).astype(BF16)
        if k + 1 < ticks:
            spread(Fl.at[k], A.at[k + 1], ("A", k + 1), s + 1, up)
        else:
            to_blocks(Fl.at[k], fin_a, ("fin_a",), s)

    def backward_gather(k):
        gather_start(U.at[k], ("U", k), None if k == 0 else s == last)

    def backward_pass_on(k):
        gather_mid(U.at[k], ("U", k))

    def backward_project(k):
        gather_end(U.at[k], ("U", k), None if k == 0 else s < last)
        part = mm(U[k], w_out[...], NT)
        xs[3 * k + 2] = part.astype(BF16)
        swap_send(3 * k + 2, ("xg", k))
        return part

    def backward_branch(k, part):
        arrived(xr.at[3 * k + 2], ("xg", k))
        grad_pre = ((part + xr[3 * k + 2].astype(F32)) * b_sg[k]).astype(BF16)
        GP[pl.ds(k * tokens, tokens)] = grad_pre
        center = jnp.sum(grad_pre.astype(F32) * b_pre[k], axis=-1, keepdims=True)
        center_hi = center.astype(BF16).astype(F32)
        lane = lax.broadcasted_iota(jnp.int32, (tokens, BLOCK), 1)
        Bp[k, :, pl.ds(half, BLOCK)] = jnp.where(lane < BLOCK // 2, center_hi, center - center_hi).astype(BF16)
        Bp[k, :, pl.ds(0, half)] = mm(grad_pre, w_in[...], NT).astype(BF16)
        sum_start(Bp.at[k], Br.at[k], bwd_width, ("B", k))

    def backward_sum(k):
        sum_mid(Bp.at[k], Br.at[k], Bs.at[k], bwd_width, ("B", k))

    def backward_leave(k):
        total = sum_end(Bp.at[k], Br.at[k], ("B", k))
        grad_normed = total[:, :half]
        center = total[:, half : half + 1] + total[:, half + BLOCK // 2 : half + BLOCK // 2 + 1]
        inv = unit_scale[k, rows_of(0)][:, 0:1]
        unit = R[k, rows_of(0)].astype(F32) * inv
        grads = grad_normed * gain[...] - unit * (center * (1.0 / model))
        Bl[k] = (U[k, rows_of(0)].astype(F32) + inv * grads).astype(BF16)
        if k + 1 < ticks:
            spread(Bl.at[k], U.at[k + 1], ("U", k + 1), s - 1, down)
        else:
            to_blocks(Bl.at[k], fin_g, ("fin_g",), s)
        terms = grad_normed * unit
        terms = terms[0:8] + terms[8:16]
        gacc[...] = terms if k == 0 else gacc[...] + terms

    def grad_out_weights():
        step = 256
        for i in range(inner // step):
            cols = pl.ds(i * step, step)
            total = mm(BH[pl.ds(0, tokens), cols], U[0], TN)
            for k in range(1, ticks):
                total = total + mm(BH[pl.ds(k * tokens, tokens), cols], U[k], TN)
            grad_out_w[0, cols, :] = (total * scale_out).astype(BF16)

    def grad_in_weights():
        step = 256
        for i in range(half // step):
            cols = pl.ds(i * step, step)
            grad_in_w[0, cols, :] = (mm(BN[:, cols], GP[...], TN) * scale_out).astype(BF16)

    def stash_out(k):
        if k == 0:
            arrived(raw.at[0], ("raw", 0))
        else:

            @pl.when(s < last)
            def _():
                arrived(raw.at[k], ("raw", k))

            @pl.when(s == last)
            def _():
                raw[k] = act_fresh[k - 1]

        quantize(k)

    for k in range(ticks):
        more = k + 1 < ticks
        forward_gather(k)
        if k == 0:
            loads[7].wait()
            loads[8].wait()
        else:
            backward_sum(k - 1)
        forward_pass_on(k)
        if k == 0:
            backward_gather(0)
            gather_start(R.at[0], ("R", 0))
            later_slots(1)
        else:
            backward_leave(k - 1)
            backward_gather(k)
            to_blocks(Fl.at[k - 1], raw.at[k], ("raw", k), last - 1 - s, up, s == last // 2)
            restore_finish(k, r_part)
        f_part = forward_project(k)
        if k > 0 and more:
            gather_start(R.at[k + 1], ("R", k + 1))
        if k == 0:
            gather_mid(R.at[0], ("R", 0))
        backward_pass_on(k)
        if not more:
            stash_out(0)
        forward_branch(k, f_part)
        if k == 0:
            gather_end(R.at[0], ("R", 0))
            r_part = restore_project(0)
            gather_start(R.at[1], ("R", 1))
        if k + 2 < ticks:
            later_slots(k + 2)
        g_part = backward_project(k)
        if not more:
            stash_out(1)
        if more:
            gather_mid(R.at[k + 1], ("R", k + 1))
        forward_sum(k)
        if k == 0:
            restore_finish(0, r_part)
        if not more:
            stash_out(2)
        backward_branch(k, g_part)
        if more:
            gather_end(R.at[k + 1], ("R", k + 1))
            r_part = restore_project(k + 1)
        else:
            grad_out_weights()
        forward_leave(k)
    backward_sum(ticks - 1)
    grad_in_weights()
    backward_leave(ticks - 1)
    for i in range(4):
        for e in range(DP):
            push(
                gacc.at[:, pl.ds(i * width + e * (width // DP), width // DP)], gpieces.at[t], ("gp",),
                dev(s, 4 * d + i, e), None, jnp.logical_and(is_own(i), d == e),
            )
    arrived(fin_a, ("fin_a",))
    act_out[0] = fin_a[...]
    arrived(fin_g, ("fin_g",))
    grad_out[0] = fin_g[...]
    arrived(gpieces, ("gp",))
    groups = [
        jnp.sum(sum(gpieces[4 * g + i] for i in range(4)), axis=0, keepdims=True).astype(BF16).astype(F32)
        for g in range(DP)
    ]
    grad_gain[...] = (groups[0] + groups[1]) * scale_out
    for copy, cond in pending:
        if cond is None:
            copy.wait_send()
        else:
            pl.when(cond)(copy.wait_send)


def store_kernel(*refs):
    count = len(refs) // 2
    copies = [pltpu.make_async_copy(refs[i], refs[count + i], refs[-1].at[i]) for i in range(count)]
    for copy in copies:
        copy.start()
    for copy in copies:
        copy.wait()


def local(act_first, act_fresh, grad_first, grad_fresh, stash_values, stash_scales, gains, w_in, w_out):
    sections = lax.axis_size("section")
    ticks = act_fresh.shape[0] + 1
    tok, width = act_first.shape[1:]
    half, inner = w_in.shape[1:]
    tokens = tok * DP
    rows = tokens // TP
    scales = jnp.swapaxes(stash_scales, 2, 3)
    vmem = pl.BlockSpec(memory_space=pltpu.VMEM)
    hbm = pl.BlockSpec(memory_space=pl.ANY)
    bw = half + BLOCK
    V = pltpu.VMEM
    outs = pl.pallas_call(
        functools.partial(kernel, sections, ticks, tok, width, half, inner),
        out_shape=(
            V(act_first.shape, BF16),
            V(grad_first.shape, BF16),
            V(stash_values.shape, BF16),
            V(scales.shape, BF16),
            V(w_in.shape, BF16),
            V(w_out.shape, BF16),
            V((1, width // DP), F32),
        ),
        in_specs=[hbm] * 9,
        out_specs=(vmem,) * 7,
        scratch_shapes=[
            V((tok, width), BF16),
            V(act_fresh.shape, BF16),
            V((tok, width), BF16),
            V(act_fresh.shape, BF16),
            V((ticks, tok, width), BF16),
            V(scales.shape[1:], BF16),
            V((1, half), F32),
            V((half, inner), BF16),
            V((inner, half), BF16),
            V((ticks, tokens, half), BF16),
            V((ticks, tokens, half), BF16),
            V((ticks, tokens, half), BF16),
            V((ticks, tok, width), BF16),
            V((ticks, tok, width), BF16),
            V((ticks, tokens, half), BF16),
            V((ticks, tokens, bw), BF16),
            V((ticks, 8, rows, half), BF16),
            V((ticks, 8, rows, bw), BF16),
            V((ticks, 2, rows, half), BF16),
            V((ticks, 2, rows, bw), BF16),
            V((ticks, rows, half), BF16),
            V((ticks, rows, half), BF16),
            V((3 * ticks, tokens, inner), BF16),
            V((3 * ticks, tokens, inner), BF16),
            V((3 * ticks, 8, tokens), F32),
            V((3 * ticks, 8, tokens), F32),
            V((ticks, tokens, inner), F32),
            V((ticks, tokens, inner), F32),
            V((ticks * tokens, half), BF16),
            V((ticks * tokens, inner), BF16),
            V((ticks * tokens, inner), BF16),
            V((ticks, tokens, BLOCK), F32),
            V((8, half), F32),
            V((TP, 8, width // DP), F32),
            V((tok, width), BF16),
            V((tok, width), BF16),
            pltpu.SemaphoreType.DMA((9,)),
            pltpu.SemaphoreType.DMA((232,)),
            pltpu.SemaphoreType.DMA((160,)),
        ],
        compiler_params=pltpu.CompilerParams(
            collective_id=1, has_side_effects=True, vmem_limit_bytes=59 * 2**20
        ),
        name="relay_window",
    )(act_first, act_fresh, grad_first, grad_fresh, stash_values, scales, gains, w_in, w_out)
    outs = list(
        pl.pallas_call(
            store_kernel,
            out_shape=tuple(jax.ShapeDtypeStruct(o.shape, o.dtype) for o in outs),
            in_specs=[vmem] * len(outs),
            out_specs=(hbm,) * len(outs),
            scratch_shapes=[pltpu.SemaphoreType.DMA((len(outs),))],
            compiler_params=pltpu.CompilerParams(vmem_limit_bytes=8 * 2**20),
            name="store",
        )(*outs)
    )
    outs[3] = jnp.swapaxes(outs[3], 2, 3)
    return tuple(outs)


def solution(mesh):
    in_specs = (
        P("section", "dp", "tp"),
        P(None, "dp", "tp"),
        P("section", "dp", "tp"),
        P(None, "dp", "tp"),
        P("section", None, "dp", "tp"),
        P("section", None, "dp", "tp"),
        P("section", None),
        P("section", "dp", "tp"),
        P("section", "tp", "dp"),
    )
    out_specs = (
        P("section", "dp", "tp"),
        P("section", "dp", "tp"),
        P("section", None, "dp", "tp"),
        P("section", None, "dp", "tp"),
        P("section", "dp", "tp"),
        P("section", "tp", "dp"),
        P("section", ("tp", "dp")),
    )
    return jax.shard_map(local, mesh=mesh, in_specs=in_specs, out_specs=out_specs, check_vma=False)
```

```python
import functools
import math

import jax
import jax.numpy as jnp
from jax import lax
from jax.experimental import pallas as pl
from jax.experimental.pallas import tpu as pltpu
from jax.sharding import PartitionSpec as P

MESH = pl.DeviceIdType.MESH
scope = jax.named_scope
BLOCK = 128
EPS = 1e-05
QUANT_TOP = 448.0
SCALE_EPS = 1e-06
F32 = jnp.float32
BF16 = jnp.bfloat16

TP = 8
DP = 2

NN = (((1,), (0,)), ((), ()))
NT = (((1,), (1,)), ((), ()))
TN = (((0,), (0,)), ((), ()))


def mm(a, b, dims):
    return lax.dot_general(a, b, dims, preferred_element_type=F32)


def sigmoid(x):
    return 1.0 / (1.0 + jnp.exp(-x))


def column_of(tile, rows):
    wide = jnp.concatenate([tile] * (rows // 8), axis=0)
    return wide.T[:, 0:1]


def tile_of(column, rows):
    return jnp.broadcast_to(column, (rows, rows)).T[0:8, :]


def kernel(
    sections, ticks, tok, width, half, inner,
    act_first_h, act_fresh_h, grad_first_h, grad_fresh_h, stash_values_h, stash_scales_h, gains_h, w_in_h, w_out_h,
    act_out, grad_out, out_values, out_scales, grad_in_w, grad_out_w, grad_gain,
    act_first, act_fresh, grad_first, grad_fresh, stash_values, stash_scales, gain, w_in, w_out,
    A, U, R, rest, raw,
    Fp, Bp, Fr, Br, Fs, Bs, Fl, Bl,
    xs, xr, xsum_s, xsum_r,
    b_pre, b_sg, BN, BH, GP, unit_scale,
    gacc, gpieces,
    fin_a, fin_g,
    lsem, ssem, rsem,
):
    s = lax.axis_index("section")
    t = lax.axis_index("tp")
    d = lax.axis_index("dp")
    tokens = DP * tok
    rows = tokens // TP
    hw = half // 2
    model = half * DP
    fwd_width, bwd_width = half, half + 128

    quarter = lax.rem(t, 4)
    side = t // 4
    last = sections - 1

    def dev(sec, tp, dp):
        return {"section": sec, "tp": tp, "dp": dp}

    def ztp(by):
        return lax.rem(t + (by + TP), TP)

    counts = {"s": 0}
    names = {}
    pending = []

    def slot(key):
        if key not in names:
            names[key] = len(names)
        return rsem.at[names[key]]

    def push(src, dst, key, device, cond=None, is_self=None):
        sem = ssem.at[counts["s"]]
        counts["s"] += 1
        arrive = slot(key)
        copy = pltpu.make_async_remote_copy(
            src_ref=src, dst_ref=dst, send_sem=sem, recv_sem=arrive, device_id=device, device_id_type=MESH
        )
        go = cond
        if is_self is not None:
            own = is_self if cond is None else jnp.logical_and(cond, is_self)
            go = jnp.logical_not(is_self) if cond is None else jnp.logical_and(cond, jnp.logical_not(is_self))

            @pl.when(own)
            def _():
                pltpu.make_async_copy(src, dst, arrive).start()

        if go is None:
            copy.start()
        else:
            pl.when(go)(copy.start)
        pending.append((copy, go))

    def arrived(ref, key):
        pltpu.make_async_copy(ref, ref, slot(key)).wait()

    loads = []
    for i, (src, dst) in enumerate(
        (
            (stash_values_h.at[0], stash_values),
            (stash_scales_h.at[0], stash_scales),
            (act_first_h.at[0], act_first),
            (grad_first_h.at[0], grad_first),
            (gains_h.at[:, pl.ds(pl.multiple_of(d * half, half), half)], gain),
            (act_fresh_h, act_fresh),
            (grad_fresh_h, grad_fresh),
            (w_in_h.at[0], w_in),
            (w_out_h.at[0], w_out),
        )
    ):
        loads.append(pltpu.make_async_copy(src, dst, lsem.at[i]))
    for load in loads:
        load.start()

    barrier = pltpu.get_barrier_semaphore()

    def greet(device, cond=None):
        def signal():
            pl.semaphore_signal(barrier, inc=1, device_id=device, device_id_type=MESH)

        if cond is None:
            signal()
        else:
            pl.when(cond)(signal)

    def is_own(i):
        return jnp.logical_and(side == d, quarter == i)

    up, down = s < last, s > 0
    for by in (1, -1, 2, -2):
        greet(dev(s, ztp(by), d))
    greet(dev(s, t, 1 - d))
    for by in (0, 1, -1, 2, -2):
        greet(dev(s + 1, ztp(by), d), up)
        greet(dev(s - 1, ztp(by), d), down)
    greet(dev(last - s, t, d))
    for i in range(4):
        greet(dev(s, 4 * d + i, side), jnp.logical_not(is_own(i)))
        greet(dev(last - s, 4 * d + i, side))
        greet(dev(last - 1 - s, 4 * d + i, side), jnp.logical_and(up, jnp.logical_not(jnp.logical_and(s == last // 2, is_own(i)))))
    for i in range(TP):
        greet(dev(s, i, side), jnp.logical_not(jnp.logical_and(side == d, t == i)))
    self_side = (side == d).astype(jnp.int32)
    expect = (
        4 + 1 + 5 * up.astype(jnp.int32) + 5 * down.astype(jnp.int32) + 1
        + (4 - self_side) + 4 + (TP - self_side)
        + up.astype(jnp.int32) * (4 - self_side * (s == last // 2).astype(jnp.int32))
    )

    loads[0].wait()
    loads[1].wait()
    blocks = width // BLOCK
    eye = (
        lax.broadcasted_iota(jnp.int32, (blocks, blocks), 0) == lax.broadcasted_iota(jnp.int32, (blocks, blocks), 1)
    ).astype(F32).astype(BF16)
    for k in range(ticks):
        scale = mm(stash_scales[k], eye, TN)
        for b in range(blocks):
            cols = pl.ds(b * BLOCK, BLOCK)
            rest[k, :, cols] = (stash_values[k, :, cols].astype(F32) * scale[:, b : b + 1]).astype(BF16)

    loads[2].wait()
    loads[3].wait()
    pl.semaphore_wait(barrier, expect)

    piece_cols = pl.ds(pl.multiple_of(quarter * width, width), width)

    def to_slots(src, dst, key, sec, cond=None, other=False):
        for i in range(4):
            push(
                src.at[pl.ds(rows * i, rows)], dst.at[pl.ds(0, rows), piece_cols], key,
                dev(sec, 4 * d + i, side), cond, None if other else is_own(i),
            )

    def to_blocks(src, dst, key, sec, cond=None, own=None):
        for i in range(4):
            mine = is_own(i) if own is None else jnp.logical_and(own, is_own(i))
            push(
                src.at[pl.ds(0, rows), pl.ds(i * width, width)],
                dst.at[pl.ds(pl.multiple_of(quarter * rows, rows), rows)], key,
                dev(sec, 4 * d + i, side), cond, mine,
            )

    to_slots(act_first, A.at[0], ("A", 0), s)
    to_slots(rest.at[0], R.at[0], ("R", 0), last - s, other=True)
    to_slots(grad_first, U.at[0], ("U", 0), s)
    loads[4].wait()
    loads[5].wait()
    loads[6].wait()

    def later_slots(k):
        to_slots(rest.at[k], R.at[k], ("R", k), last - s, other=True)
        to_slots(act_fresh.at[k - 1], A.at[k], ("A", k), s, s == 0)
        to_slots(grad_fresh.at[k - 1], U.at[k], ("U", k), s, s == last)
        if k == 1:
            push(act_first, raw.at[0], ("raw", 0), dev(last - s, t, d))

    def rows_of(j):
        return pl.ds(rows * j, rows)

    def spread(src, X, key, sec, cond=None, whole=True):
        push(src, X.at[rows_of(2)], key + (2,), dev(sec, ztp(-2), d), cond)
        push(src, X.at[rows_of(6)], key + (6,), dev(sec, ztp(2), d), cond)
        push(src, X.at[rows_of(1)], key + (1,), dev(sec, ztp(-1), d), cond)
        push(src, X.at[rows_of(7)], key + (7,), dev(sec, ztp(1), d), cond)
        if whole:
            push(src, X.at[rows_of(0)], key, dev(sec, t, d), cond)

    def gather_start(X, key, cond=None):
        def first():
            arrived(X.at[rows_of(0)], key)

        if cond is None:
            first()
        else:
            pl.when(cond)(first)
        spread(X.at[rows_of(0)], X, key, s, cond, False)

    def chain(X, key, step):
        if step == 0:
            arrived(X.at[rows_of(0)], key)
            push(X.at[rows_of(0)], X.at[rows_of(1)], key + (1,), dev(s, ztp(-1), d))
            push(X.at[rows_of(0)], X.at[rows_of(7)], key + (7,), dev(s, ztp(1), d))
        elif step < 3:
            arrived(X.at[rows_of(step)], key + (step,))
            push(X.at[rows_of(step)], X.at[rows_of(step + 1)], key + (step + 1,), dev(s, ztp(-1), d))
            arrived(X.at[rows_of(8 - step)], key + (8 - step,))
            push(X.at[rows_of(8 - step)], X.at[rows_of(7 - step)], key + (7 - step,), dev(s, ztp(1), d))
        elif step == 3:
            arrived(X.at[rows_of(3)], key + (3,))
            push(X.at[rows_of(3), pl.ds(0, hw)], X.at[rows_of(4), pl.ds(0, hw)], key + (4,), dev(s, ztp(-1), d))
            arrived(X.at[rows_of(5)], key + (5,))
            push(X.at[rows_of(5), pl.ds(hw, hw)], X.at[rows_of(4), pl.ds(hw, hw)], key + (8,), dev(s, ztp(1), d))
        else:
            arrived(X.at[rows_of(4), pl.ds(0, hw)], key + (4,))
            arrived(X.at[rows_of(4), pl.ds(hw, hw)], key + (8,))

    def gather_mid(X, key):
        arrived(X.at[rows_of(2)], key + (2,))
        push(X.at[rows_of(2)], X.at[rows_of(3)], key + (3,), dev(s, ztp(-1), d))
        push(X.at[rows_of(2), pl.ds(0, hw)], X.at[rows_of(4), pl.ds(0, hw)], key + (4,), dev(s, ztp(-2), d))
        arrived(X.at[rows_of(6)], key + (6,))
        push(X.at[rows_of(6)], X.at[rows_of(5)], key + (5,), dev(s, ztp(1), d))
        push(X.at[rows_of(6), pl.ds(hw, hw)], X.at[rows_of(4), pl.ds(hw, hw)], key + (8,), dev(s, ztp(2), d))

    def gather_end(X, key, cond=None):
        if cond is not None:
            pl.when(cond)(lambda: arrived(X.at[rows_of(0)], key))
        for j in (1, 7, 3, 5):
            arrived(X.at[rows_of(j)], key + (j,))
        arrived(X.at[rows_of(4), pl.ds(0, hw)], key + (4,))
        arrived(X.at[rows_of(4), pl.ds(hw, hw)], key + (8,))

    def sum_start(Pk, Rk, w, key):
        push(Pk.at[rows_of(3)], Rk.at[0], key + (0,), dev(s, ztp(1), d))
        push(Pk.at[rows_of(5)], Rk.at[1], key + (1,), dev(s, ztp(-1), d))
        push(Pk.at[rows_of(4), pl.ds(0, hw)], Rk.at[2, :, pl.ds(0, hw)], key + (2,), dev(s, ztp(2), d))
        push(Pk.at[rows_of(4), pl.ds(hw, w - hw)], Rk.at[3, :, pl.ds(hw, w - hw)], key + (3,), dev(s, ztp(-2), d))
        push(Pk.at[rows_of(1)], Rk.at[4], key + (4,), dev(s, ztp(1), d))
        push(Pk.at[rows_of(7)], Rk.at[5], key + (5,), dev(s, ztp(-1), d))

    def sum_mid(Pk, Rk, Sk, w, key):
        arrived(Rk.at[0], key + (0,))
        arrived(Rk.at[2, :, pl.ds(0, hw)], key + (2,))
        lo, hi = pl.ds(0, hw), pl.ds(hw, w - hw)
        Sk[0, :, lo] = (
            Pk[rows_of(2), lo].astype(F32) + Rk[0, :, lo].astype(F32) + Rk[2, :, lo].astype(F32)
        ).astype(BF16)
        Sk[0, :, hi] = (Pk[rows_of(2), hi].astype(F32) + Rk[0, :, hi].astype(F32)).astype(BF16)
        push(Sk.at[0], Rk.at[6], key + (6,), dev(s, ztp(2), d))
        arrived(Rk.at[1], key + (1,))
        arrived(Rk.at[3, :, pl.ds(hw, w - hw)], key + (3,))
        Sk[1, :, hi] = (
            Pk[rows_of(6), hi].astype(F32) + Rk[1, :, hi].astype(F32) + Rk[3, :, hi].astype(F32)
        ).astype(BF16)
        Sk[1, :, lo] = (Pk[rows_of(6), lo].astype(F32) + Rk[1, :, lo].astype(F32)).astype(BF16)
        push(Sk.at[1], Rk.at[7], key + (7,), dev(s, ztp(-2), d))

    def sum_end(Pk, Rk, key):
        for j in (4, 5, 6, 7):
            arrived(Rk.at[j], key + (j,))
        total = Pk[rows_of(0)].astype(F32)
        for j in (4, 5, 6, 7):
            total = total + Rk[j].astype(F32)
        return total

    def swap_send(i, key):
        push(xs.at[i], xr.at[i], key, dev(s, t, 1 - d))

    def swap_sum_send(i, key):
        push(xsum_s.at[i], xsum_r.at[i], key + ("q",), dev(s, t, 1 - d))

    def project(X, i, key):
        wide = X[...].astype(F32)
        xsum_s[i] = tile_of(jnp.sum(wide * wide, axis=-1, keepdims=True), tokens)
        swap_sum_send(i, key)
        part = mm((wide * gain[...]).astype(BF16), w_in[...], NN)
        xs[i] = part.astype(BF16)
        swap_send(i, key)
        return part

    def projected(part, i, key):
        arrived(xsum_r.at[i], key + ("q",))
        arrived(xr.at[i], key)
        total = column_of(xsum_s[i] + xsum_r[i], tokens)
        inv = lax.rsqrt(total * (1.0 / model) + EPS)
        return inv * (part + xr[i].astype(F32)), inv

    def restore_project(k):
        return project(R.at[k], 3 * k + 1, ("xb", k))

    def restore_finish(k, part):
        pre, inv = projected(part, 3 * k + 1, ("xb", k))
        gate = sigmoid(pre)
        unit_scale[k] = jnp.broadcast_to(inv, (tokens, BLOCK))
        b_pre[k] = pre
        b_sg[k] = gate * (1.0 + pre * (1.0 - gate))
        BH[pl.ds(k * tokens, tokens)] = (pre * gate).astype(BF16)
        BN[pl.ds(k * tokens, tokens)] = (R[k].astype(F32) * inv * gain[...]).astype(BF16)

    def quantize(k):
        values = raw[k].astype(F32)
        scales = []
        for b in range(width // BLOCK):
            block = values[:, b * BLOCK : (b + 1) * BLOCK]
            top = jnp.max(jnp.abs(block), axis=-1, keepdims=True)
            scale = (top / QUANT_TOP + SCALE_EPS).astype(BF16)
            out_values[0, k, :, pl.ds(b * BLOCK, BLOCK)] = (block / scale.astype(F32)).astype(BF16)
            scales.append(scale.astype(F32))
        out_scales[0, k] = mm(eye, jnp.concatenate(scales, axis=1).astype(BF16), NT).astype(BF16)

    scale_out = 1.0 / math.sqrt(ticks * tokens)

    def forward_gather(k):
        gather_start(A.at[k], ("A", k), None if k == 0 else s == 0)

    def forward_pass_on(k):
        gather_mid(A.at[k], ("A", k))

    def forward_project(k):
        gather_end(A.at[k], ("A", k), None if k == 0 else s > 0)
        return project(A.at[k], 3 * k, ("xf", k))

    def forward_branch(k, part):
        pre, _ = projected(part, 3 * k, ("xf", k))
        hidden = (pre * sigmoid(pre)).astype(BF16)
        Fp[k] = mm(hidden, w_out[...], NN).astype(BF16)
        sum_start(Fp.at[k], Fr.at[k], fwd_width, ("F", k))

    def forward_sum(k):
        sum_mid(Fp.at[k], Fr.at[k], Fs.at[k], fwd_width, ("F", k))

    def forward_leave(k):
        Fl[k] = (A[k, rows_of(0)].astype(F32) + sum_end(Fp.at[k], Fr.at[k], ("F", k))).astype(BF16)
        if k + 1 < ticks:
            spread(Fl.at[k], A.at[k + 1], ("A", k + 1), s + 1, up)
        else:
            to_blocks(Fl.at[k], fin_a, ("fin_a",), s)

    def backward_gather(k):
        gather_start(U.at[k], ("U", k), None if k == 0 else s == last)

    def backward_pass_on(k):
        gather_mid(U.at[k], ("U", k))

    def backward_project(k):
        gather_end(U.at[k], ("U", k), None if k == 0 else s < last)
        part = mm(U[k], w_out[...], NT)
        xs[3 * k + 2] = part.astype(BF16)
        swap_send(3 * k + 2, ("xg", k))
        return part

    def backward_branch(k, part):
        arrived(xr.at[3 * k + 2], ("xg", k))
        grad_pre = ((part + xr[3 * k + 2].astype(F32)) * b_sg[k]).astype(BF16)
        GP[pl.ds(k * tokens, tokens)] = grad_pre
        center = jnp.sum(grad_pre.astype(F32) * b_pre[k], axis=-1, keepdims=True)
        center_hi = center.astype(BF16).astype(F32)
        lane = lax.broadcasted_iota(jnp.int32, (tokens, BLOCK), 1)
        Bp[k, :, pl.ds(half, BLOCK)] = jnp.where(lane < BLOCK // 2, center_hi, center - center_hi).astype(BF16)
        Bp[k, :, pl.ds(0, half)] = mm(grad_pre, w_in[...], NT).astype(BF16)
        sum_start(Bp.at[k], Br.at[k], bwd_width, ("B", k))

    def backward_sum(k):
        sum_mid(Bp.at[k], Br.at[k], Bs.at[k], bwd_width, ("B", k))

    def backward_leave(k):
        total = sum_end(Bp.at[k], Br.at[k], ("B", k))
        grad_normed = total[:, :half]
        center = total[:, half : half + 1] + total[:, half + BLOCK // 2 : half + BLOCK // 2 + 1]
        inv = unit_scale[k, rows_of(0)][:, 0:1]
        unit = R[k, rows_of(0)].astype(F32) * inv
        grads = grad_normed * gain[...] - unit * (center * (1.0 / model))
        Bl[k] = (U[k, rows_of(0)].astype(F32) + inv * grads).astype(BF16)
        if k + 1 < ticks:
            spread(Bl.at[k], U.at[k + 1], ("U", k + 1), s - 1, down)
        else:
            to_blocks(Bl.at[k], fin_g, ("fin_g",), s)
        terms = grad_normed * unit
        terms = terms[0:8] + terms[8:16]
        gacc[...] = terms if k == 0 else gacc[...] + terms

    def grad_out_weights():
        step = 256
        for i in range(inner // step):
            cols = pl.ds(i * step, step)
            total = mm(BH[pl.ds(0, tokens), cols], U[0], TN)
            for k in range(1, ticks):
                total = total + mm(BH[pl.ds(k * tokens, tokens), cols], U[k], TN)
            grad_out_w[0, cols, :] = (total * scale_out).astype(BF16)

    def grad_in_weights():
        step = 256
        for i in range(half // step):
            cols = pl.ds(i * step, step)
            grad_in_w[0, cols, :] = (mm(BN[:, cols], GP[...], TN) * scale_out).astype(BF16)

    def stash_out(k):
        if k == 0:
            arrived(raw.at[0], ("raw", 0))
        else:

            @pl.when(s < last)
            def _():
                arrived(raw.at[k], ("raw", k))

            @pl.when(s == last)
            def _():
                raw[k] = act_fresh[k - 1]

        quantize(k)

    for k in range(ticks):
        more = k + 1 < ticks
        forward_gather(k)
        if k == 0:
            loads[7].wait()
            loads[8].wait()
        else:
            backward_sum(k - 1)
            chain(R.at[k], ("R", k), 2)
        forward_pass_on(k)
        if k == 0:
            backward_gather(0)
            gather_start(R.at[0], ("R", 0))
            later_slots(1)
        else:
            backward_leave(k - 1)
            backward_gather(k)
            to_blocks(Fl.at[k - 1], raw.at[k], ("raw", k), last - 1 - s, up, s == last // 2)
            chain(R.at[k], ("R", k), 3)
        f_part = forward_project(k)
        if k > 0:
            chain(R.at[k], ("R", k), 4)
            r_part = restore_project(k)
        if k == 0:
            gather_mid(R.at[0], ("R", 0))
        backward_pass_on(k)
        if not more:
            stash_out(0)
        forward_branch(k, f_part)
        if k > 0:
            restore_finish(k, r_part)
        if k == 0:
            gather_end(R.at[0], ("R", 0))
            r_part = restore_project(0)
        if k + 2 < ticks:
            later_slots(k + 2)
        g_part = backward_project(k)
        if not more:
            stash_out(1)
        forward_sum(k)
        if k == 0:
            restore_finish(0, r_part)
        if not more:
            stash_out(2)
        backward_branch(k, g_part)
        if more:
            chain(R.at[k + 1], ("R", k + 1), 0)
        else:
            grad_out_weights()
        forward_leave(k)
        if more:
            chain(R.at[k + 1], ("R", k + 1), 1)
    backward_sum(ticks - 1)
    grad_in_weights()
    backward_leave(ticks - 1)
    for i in range(4):
        for e in range(DP):
            push(
                gacc.at[:, pl.ds(i * width + e * (width // DP), width // DP)], gpieces.at[t], ("gp",),
                dev(s, 4 * d + i, e), None, jnp.logical_and(is_own(i), d == e),
            )
    arrived(fin_a, ("fin_a",))
    act_out[0] = fin_a[...]
    arrived(fin_g, ("fin_g",))
    grad_out[0] = fin_g[...]
    arrived(gpieces, ("gp",))
    groups = [
        jnp.sum(sum(gpieces[4 * g + i] for i in range(4)), axis=0, keepdims=True).astype(BF16).astype(F32)
        for g in range(DP)
    ]
    grad_gain[...] = (groups[0] + groups[1]) * scale_out
    for copy, cond in pending:
        if cond is None:
            copy.wait_send()
        else:
            pl.when(cond)(copy.wait_send)


def store_kernel(*refs):
    count = len(refs) // 2
    copies = [pltpu.make_async_copy(refs[i], refs[count + i], refs[-1].at[i]) for i in range(count)]
    for copy in copies:
        copy.start()
    for copy in copies:
        copy.wait()


def local(act_first, act_fresh, grad_first, grad_fresh, stash_values, stash_scales, gains, w_in, w_out):
    sections = lax.axis_size("section")
    ticks = act_fresh.shape[0] + 1
    tok, width = act_first.shape[1:]
    half, inner = w_in.shape[1:]
    tokens = tok * DP
    rows = tokens // TP
    scales = jnp.swapaxes(stash_scales, 2, 3)
    vmem = pl.BlockSpec(memory_space=pltpu.VMEM)
    hbm = pl.BlockSpec(memory_space=pl.ANY)
    bw = half + BLOCK
    V = pltpu.VMEM
    outs = pl.pallas_call(
        functools.partial(kernel, sections, ticks, tok, width, half, inner),
        out_shape=(
            V(act_first.shape, BF16),
            V(grad_first.shape, BF16),
            V(stash_values.shape, BF16),
            V(scales.shape, BF16),
            V(w_in.shape, BF16),
            V(w_out.shape, BF16),
            V((1, width // DP), F32),
        ),
        in_specs=[hbm] * 9,
        out_specs=(vmem,) * 7,
        scratch_shapes=[
            V((tok, width), BF16),
            V(act_fresh.shape, BF16),
            V((tok, width), BF16),
            V(act_fresh.shape, BF16),
            V((ticks, tok, width), BF16),
            V(scales.shape[1:], BF16),
            V((1, half), F32),
            V((half, inner), BF16),
            V((inner, half), BF16),
            V((ticks, tokens, half), BF16),
            V((ticks, tokens, half), BF16),
            V((ticks, tokens, half), BF16),
            V((ticks, tok, width), BF16),
            V((ticks, tok, width), BF16),
            V((ticks, tokens, half), BF16),
            V((ticks, tokens, bw), BF16),
            V((ticks, 8, rows, half), BF16),
            V((ticks, 8, rows, bw), BF16),
            V((ticks, 2, rows, half), BF16),
            V((ticks, 2, rows, bw), BF16),
            V((ticks, rows, half), BF16),
            V((ticks, rows, half), BF16),
            V((3 * ticks, tokens, inner), BF16),
            V((3 * ticks, tokens, inner), BF16),
            V((3 * ticks, 8, tokens), F32),
            V((3 * ticks, 8, tokens), F32),
            V((ticks, tokens, inner), F32),
            V((ticks, tokens, inner), F32),
            V((ticks * tokens, half), BF16),
            V((ticks * tokens, inner), BF16),
            V((ticks * tokens, inner), BF16),
            V((ticks, tokens, BLOCK), F32),
            V((8, half), F32),
            V((TP, 8, width // DP), F32),
            V((tok, width), BF16),
            V((tok, width), BF16),
            pltpu.SemaphoreType.DMA((9,)),
            pltpu.SemaphoreType.DMA((232,)),
            pltpu.SemaphoreType.DMA((160,)),
        ],
        compiler_params=pltpu.CompilerParams(
            collective_id=1, has_side_effects=True, vmem_limit_bytes=59 * 2**20
        ),
        name="relay_window",
    )(act_first, act_fresh, grad_first, grad_fresh, stash_values, scales, gains, w_in, w_out)
    outs = list(
        pl.pallas_call(
            store_kernel,
            out_shape=tuple(jax.ShapeDtypeStruct(o.shape, o.dtype) for o in outs),
            in_specs=[vmem] * len(outs),
            out_specs=(hbm,) * len(outs),
            scratch_shapes=[pltpu.SemaphoreType.DMA((len(outs),))],
            compiler_params=pltpu.CompilerParams(vmem_limit_bytes=8 * 2**20),
            name="store",
        )(*outs)
    )
    outs[3] = jnp.swapaxes(outs[3], 2, 3)
    return tuple(outs)


def solution(mesh):
    in_specs = (
        P("section", "dp", "tp"),
        P(None, "dp", "tp"),
        P("section", "dp", "tp"),
        P(None, "dp", "tp"),
        P("section", None, "dp", "tp"),
        P("section", None, "dp", "tp"),
        P("section", None),
        P("section", "dp", "tp"),
        P("section", "tp", "dp"),
    )
    out_specs = (
        P("section", "dp", "tp"),
        P("section", "dp", "tp"),
        P("section", None, "dp", "tp"),
        P("section", None, "dp", "tp"),
        P("section", "dp", "tp"),
        P("section", "tp", "dp"),
        P("section", ("tp", "dp")),
    )
    return jax.shard_map(local, mesh=mesh, in_specs=in_specs, out_specs=out_specs, check_vma=False)
```
